32 devices in a mesh: groups: 2 (over y), blk: 4 (over z), pair: 2 (over x), sub: 2 (over core).
Axes of the slice: x: 2, y: 2, z: 4, core: 2. Of those that a mesh axis runs over, the one named last changes fastest.
Arguments:
- generated: bfloat16 [4096, 512], P(('groups', 'blk', 'pair', 'sub')), parts along dimension 0, may hold values from -16 to 16, as said below
- real: bfloat16 [512, 512], P(('groups', 'blk', 'pair', 'sub')), parts along dimension 0, may hold values from -16 to 16, as said below
Outputs:
- gradient: float32 [4096, 512], P(('groups', 'blk', 'pair', 'sub')), parts along dimension 0
- loss: float32 [2], P('groups'), parts along dimension 0
The draws below stay inside these ranges and needn't reach their ends.
There are 2 independent parts, one for each index of `groups`. The reference program is written for one: setup_inputs(seed, part) draws one part's arguments, and reference() takes and returns one part's arrays. A program takes and returns all parts, laid end to end along the dimension named above; each array names one. Nothing has to cross between parts.
Inputs may be any that keep to these rules, and one draw needn't show every extreme that they name: `generated`: generated latents, no further structure promised. `real`: real latents, no further structure promised.
All inputs are finite; a program needn't handle non-finite values.
Results may differ from the reference program's by a relative error of at most 0.0023.
Values may be sent and summed in bfloat16 or wider, within the bound.
No kernel may reach another device: no remote copies, remote signals or barrier semaphores. Data moves between devices by JAX's collectives and lax.ppermute only.
A program may use at most 64 MiB of HBM per device.

```python
import jax
import jax.numpy as jnp
from jax import lax

D = 512
G_DEV = 128
NG = 2048
NR = 256
N_PAIR = 2
N_SUB = 2


cluster_count = 24


factor_rank = 16


def shared_mixture(key):
    key_mean, key_load, key_size, key_amp = jax.random.split(key, 4)
    mean_size = jnp.exp(jax.random.uniform(key_size, (cluster_count, 1), jnp.float32, jnp.log(0.3), jnp.log(1.5)))
    cluster_mean = jax.random.truncated_normal(key_mean, -3.0, 3.0, (cluster_count, D), jnp.float32) * mean_size
    loadings = jax.random.truncated_normal(key_load, -3.0, 3.0, (cluster_count, factor_rank, D), jnp.float32) * 0.25
    amplitude = jnp.exp(jax.random.uniform(key_amp, (cluster_count, 1), jnp.float32, jnp.log(0.2), jnp.log(1.0)))
    return (cluster_mean, loadings, amplitude)


def assemble(cluster, factors, noise_part, cluster_mean, loadings, amplitude):
    row_count = cluster.shape[0]
    shape_part = jnp.zeros((row_count, loadings.shape[2]), jnp.float32)
    for factor_index in range(factor_rank):
        picked = jnp.take(loadings[:, factor_index, :], cluster, axis=0)
        shape_part = shape_part + factors[:, factor_index:factor_index + 1] * picked
    rising = jnp.exp(jnp.log(3.0) * jnp.arange(row_count, dtype=jnp.float32) / max(row_count - 1, 1))[:, None]
    centre = jnp.take(cluster_mean, cluster, axis=0)
    spread = jnp.take(amplitude, cluster, axis=0)
    return rising * (centre + (spread * shape_part + noise_part))


def draw_generated(key, part):
    cluster_mean, loadings, amplitude = shared_mixture(key)
    key = jax.random.fold_in(key, 11)
    key_id, key_factor, key_noise, key_shift = jax.random.split(key, 4)
    cluster = jax.random.randint(key_id, (NG,), 0, cluster_count)
    cluster_mean = cluster_mean + jax.random.truncated_normal(key_shift, -3.0, 3.0, (cluster_count, D), jnp.float32) * 0.3
    factors = jax.random.truncated_normal(key_factor, -4.0, 4.0, (NG, factor_rank), jnp.float32)
    noise_part = jax.random.truncated_normal(key_noise, -4.0, 4.0, (NG, D), jnp.float32) * 0.15
    values = assemble(cluster, factors, noise_part, cluster_mean, loadings, amplitude)
    return jnp.clip(values, -16.0, 16.0).astype(jnp.bfloat16)


def draw_real(key, part):
    cluster_mean, loadings, amplitude = shared_mixture(key)
    key = jax.random.fold_in(key, 12)
    key_id, key_factor, key_noise = jax.random.split(key, 3)
    cluster = jax.random.randint(key_id, (NR,), 0, cluster_count)
    factors = jax.random.truncated_normal(key_factor, -4.0, 4.0, (NR, factor_rank), jnp.float32)
    noise_part = jax.random.truncated_normal(key_noise, -4.0, 4.0, (NR, D), jnp.float32) * 0.2
    values = assemble(cluster, factors, noise_part, cluster_mean, loadings, amplitude)
    return jnp.clip(values, -16.0, 16.0).astype(jnp.bfloat16)


def setup_inputs(seed: int = 0, part: int = 0) -> dict:
    arg_keys = jax.random.split(jax.random.key(seed), 3)
    own_keys = jax.random.split(jax.random.fold_in(arg_keys[2], part), 3)
    return {
        "generated": draw_generated(jax.random.fold_in(jax.random.fold_in(arg_keys[2], part), 71), part),
        "real": draw_real(jax.random.fold_in(jax.random.fold_in(arg_keys[2], part), 71), part),
    }


def pair_dist(rows, rows_sq, others, others_sq, width):
    gram = lax.dot_general(rows, others, (((1,), (1,)), ((), ())), preferred_element_type=jnp.float32)
    spread = jnp.maximum(rows_sq[:, None] + others_sq[None, :] - 2.0 * gram, 0.0)
    return jnp.sqrt(spread / width + 1.0)

def reference(generated, real):
    width = generated.shape[1]
    count_g = generated.shape[0]
    count_r = real.shape[0]
    gen_sq = lax.optimization_barrier(jnp.sum(jnp.square(generated.astype(jnp.float32)), axis=1))
    real_sq = lax.optimization_barrier(jnp.sum(jnp.square(real.astype(jnp.float32)), axis=1))
    rows = G_DEV * N_PAIR * N_SUB
    blocks = generated.reshape(count_g // rows, rows, width)
    block_sq = gen_sq.reshape(count_g // rows, rows)

    def one_block(item):
        block, bsq = item
        own = block.astype(jnp.float32)
        dist_g = pair_dist(block, bsq, generated, gen_sq, width)
        dist_r = pair_dist(block, bsq, real, real_sq, width)
        weight_g = 1.0 / dist_g
        weight_r = 1.0 / dist_r
        pulled_g = jnp.dot(weight_g.astype(jnp.bfloat16), generated, preferred_element_type=jnp.float32)
        pulled_r = jnp.dot(weight_r.astype(jnp.bfloat16), real, preferred_element_type=jnp.float32)
        term_g = (own * lax.optimization_barrier(jnp.sum(weight_g, axis=1))[:, None] - pulled_g) / count_g
        term_r = (own * lax.optimization_barrier(jnp.sum(weight_r, axis=1))[:, None] - pulled_r) / count_r
        partial_loss = 2.0 * jnp.sum(dist_r) / (count_g * count_r) - jnp.sum(dist_g) / (count_g * count_g)
        return (term_r - term_g, partial_loss)
    grads, parts = lax.map(one_block, (blocks, block_sq))
    return (grads.reshape(count_g, width), jnp.sum(parts).reshape(1))
```

```python
import functools

import jax
import jax.numpy as jnp
from jax import lax
from jax.experimental import pallas as pl
from jax.experimental.pallas import tpu as pltpu
from jax.sharding import PartitionSpec as P

AXES = ("blk", "pair", "sub")
EVEN_ORDER = (("pair", 1), ("blk", 2), ("blk", 1))
ODD_ORDER = (("blk", 2), ("blk", 1), ("pair", 1))
CHIP = (("sub", 1),)


def swap_pairs(sizes, even_moves, odd_moves):
    blk, pair, sub = sizes
    pairs = []
    for z in range(blk):
        for x in range(pair):
            for s in range(sub):
                at = {"blk": z, "pair": x, "sub": s}
                for axis, flip in odd_moves if s else even_moves:
                    at[axis] ^= flip
                source = (z * pair + x) * sub + s
                target = (at["blk"] * pair + at["pair"]) * sub + at["sub"]
                pairs.append((source, target))
    return pairs


def swapped(block, sizes, even_moves, odd_moves):
    return lax.ppermute(block, AXES, swap_pairs(sizes, even_moves, odd_moves))


def gathered_blocks(own, sizes):
    def step(block, index):
        return swapped(block, sizes, EVEN_ORDER[index : index + 1], ODD_ORDER[index : index + 1])

    first = step(own, 0)
    second = step(own, 1)
    third = step(own, 2)
    first_second = step(first, 1)
    first_third = step(first, 2)
    second_third = step(second, 2)
    all_three = step(first_second, 2)
    lane = [own, first, second, third, first_second, first_third, second_third, all_three]
    return [(block, swapped(block, sizes, CHIP, CHIP)) for block in lane]


def whole_kernel(g_rows, ratio, inv_total, *refs):
    n_blocks = len(refs) - 6
    blocks = refs[:n_blocks]
    grad_ref, loss_ref, ws, ncol, nrow, pulled = refs[n_blocks:]
    width = ws.shape[1]
    r_rows = blocks[0].shape[0] - g_rows
    gens = g_rows * n_blocks
    tile = 2 * g_rows
    scale = jnp.asarray(-2.0 / width, jnp.bfloat16)
    eye = lax.broadcasted_iota(jnp.int32, (g_rows, g_rows), 0) == lax.broadcasted_iota(
        jnp.int32, (g_rows, g_rows), 1
    )

    def put_norms(row, count, value):
        v = value.astype(jnp.float32)
        n = jnp.sum(v * v, axis=1, keepdims=True) * (1.0 / width) + 0.5
        ncol[pl.ds(row, count), :] = jnp.broadcast_to(n, (count, 128))

    for i, block in enumerate(blocks):
        g = block[0:g_rows, :]
        r = block[g_rows : g_rows + r_rows, :]
        ws[i * g_rows : (i + 1) * g_rows, :] = g
        ws[gens + i * r_rows : gens + (i + 1) * r_rows, :] = r
        put_norms(i * g_rows, g_rows, g)
        put_norms(gens + i * r_rows, r_rows, r)
    for i in range(ws.shape[0] // g_rows):
        n = ncol[i * g_rows : (i + 1) * g_rows, :]
        row = jnp.sum(jnp.where(eye, n, 0.0), axis=0, keepdims=True)
        q, half = divmod(i, 2)
        nrow[q, :, half * g_rows : (half + 1) * g_rows] = jnp.broadcast_to(row, (8, g_rows))

    own = ws[0:g_rows, :] * scale
    own_n = ncol[0:g_rows, :]
    pulled[...] = jnp.zeros_like(pulled)

    def spread_of(lhs, lhs_n, q):
        rhs = ws[pl.ds(pl.multiple_of(q * tile, tile), tile), :]
        c = lax.dot_general(lhs, rhs, (((1,), (1,)), ((), ())), preferred_element_type=jnp.float32)
        n = jnp.concatenate([lhs_n, lhs_n], axis=1)
        rows = c.shape[0]
        nr = nrow[q]
        nr = jnp.broadcast_to(nr[None], (rows // 8, 8, tile)).reshape(rows, tile)
        return jnp.maximum((n + nr) + c, 1.0)

    def own_step(q, carry):
        w = lax.rsqrt(spread_of(own, own_n, q))
        sign = jnp.where(q * tile < gens, 1.0, -ratio)
        w = w * sign
        rhs = ws[pl.ds(pl.multiple_of(q * tile, tile), tile), :]
        pulled[...] += jnp.dot(w.astype(jnp.bfloat16), rhs, preferred_element_type=jnp.float32)
        return carry + w[:, 0:128] + w[:, 128:256]

    w_sum = lax.fori_loop(0, ws.shape[0] // tile, own_step, jnp.zeros((g_rows, 128), jnp.float32))
    w_sum = jnp.sum(w_sum, axis=1, keepdims=True)
    grad_ref[...] = (pulled[...] - ws[0:g_rows, :].astype(jnp.float32) * w_sum) * inv_total

    def tile_sum(p, q):
        at = pl.ds(pl.multiple_of(p * tile, tile), tile)
        s = spread_of(ws[at, :] * scale, ncol[at, :], q)
        d = s * lax.rsqrt(s)
        return jnp.sum(d.reshape(tile // 8, 8, tile), axis=0)

    def column(q, acc):
        def row(p, acc):
            return acc + tile_sum(p, q) * jnp.where(p == q, -1.0, -2.0)

        acc = lax.fori_loop(0, q + 1, row, acc)
        return acc + tile_sum(gens // tile, q) * (2.0 * ratio)

    acc = lax.fori_loop(0, gens // tile, column, jnp.zeros((8, tile), jnp.float32))
    loss_ref[0] = jnp.sum(acc) * (inv_total * inv_total)


def small_shards(sizes, generated, real):
    g_rows, width = generated.shape
    r_rows = real.shape[0]
    own = jnp.concatenate([generated, real], axis=0)
    blocks = [block for both in gathered_blocks(own, sizes) for block in both]
    n = len(blocks)
    total = g_rows * n
    rows = (g_rows + r_rows) * n
    kernel = functools.partial(whole_kernel, g_rows, float(g_rows / r_rows), 1.0 / total)
    vmem = pl.BlockSpec(memory_space=pltpu.VMEM)
    grad, loss = pl.pallas_call(
        kernel,
        out_shape=(
            jax.ShapeDtypeStruct((g_rows, width), jnp.float32),
            jax.ShapeDtypeStruct((1,), jnp.float32),
        ),
        in_specs=[vmem] * n,
        out_specs=(vmem, pl.BlockSpec(memory_space=pltpu.SMEM)),
        scratch_shapes=[
            pltpu.VMEM((rows, width), jnp.bfloat16),
            pltpu.VMEM((rows, 128), jnp.float32),
            pltpu.VMEM((rows // (2 * g_rows), 8, 2 * g_rows), jnp.float32),
            pltpu.VMEM((g_rows, width), jnp.float32),
        ],
        compiler_params=pltpu.CompilerParams(vmem_limit_bytes=32 * 1024 * 1024),
    )(*blocks)
    return grad, loss


def passed_along(shard, axis, by):
    size = lax.axis_size(axis)
    return lax.ppermute(shard, axis, [(i, (i + by) % size) for i in range(size)])


def pair_dist(home, home_sq, other):
    other_sq = jnp.sum(jnp.square(other.astype(jnp.float32)), axis=1)
    gram = lax.dot_general(
        home, other, (((1,), (1,)), ((), ())), preferred_element_type=jnp.float32
    )
    spread = jnp.maximum(home_sq[:, None] + other_sq[None, :] - 2.0 * gram, 0.0)
    return jnp.sqrt(spread / home.shape[1] + 1.0)


def home_term(home, dist, other, factor):
    weight = 1.0 / dist
    pulled = jnp.dot(weight.astype(jnp.bfloat16), other, preferred_element_type=jnp.float32)
    return (factor * (home.astype(jnp.float32) * jnp.sum(weight, axis=1)[:, None] - pulled), weight)


def other_term(home, weight, other, factor):
    pulled = lax.dot_general(
        weight.astype(jnp.bfloat16),
        home,
        (((0,), (0,)), ((), ())),
        preferred_element_type=jnp.float32,
    )
    return factor * (other.astype(jnp.float32) * jnp.sum(weight, axis=0)[:, None] - pulled)


def large_shards(generated, real):
    cycle_size = lax.axis_size("blk")
    half_way = cycle_size // 2
    devices_all = lax.axis_size(("blk", "pair", "sub"))
    inv_g = 1.0 / (generated.shape[0] * devices_all)
    inv_r = 1.0 / (real.shape[0] * devices_all)
    home = lax.all_gather(generated, ("pair", "sub"), axis=0, tiled=True)
    home_sq = jnp.sum(jnp.square(home.astype(jnp.float32)), axis=1)
    dist = pair_dist(home, home_sq, generated)
    sums, weight = home_term(home, dist, generated, -inv_g)
    loss_part = -jnp.sum(dist) * inv_g * inv_g

    def sym_step(index, carry):
        visitor, partner, acc_sums, acc_loss = carry
        visitor = passed_along(visitor, "blk", 1)
        step_dist = pair_dist(home, home_sq, visitor)
        term, step_weight = home_term(home, step_dist, visitor, -inv_g)
        partner = partner + other_term(home, step_weight, visitor, -inv_g)
        partner = passed_along(partner, "blk", 1)
        return (
            visitor,
            partner,
            acc_sums + term,
            acc_loss - 2.0 * jnp.sum(step_dist) * inv_g * inv_g,
        )

    start_partner = jnp.zeros(generated.shape, jnp.float32)
    visitor, partner, sums, loss_part = lax.fori_loop(
        0, half_way - 1, sym_step, (generated, start_partner, sums, loss_part)
    )
    visitor = passed_along(visitor, "blk", 1)
    last_dist = pair_dist(home, home_sq, visitor)
    term, last_weight = home_term(home, last_dist, visitor, -inv_g)
    sums = sums + term
    loss_part = loss_part - jnp.sum(last_dist) * inv_g * inv_g
    partner = passed_along(partner, "blk", cycle_size - half_way)
    carry = (sums, loss_part)
    piece = lax.all_gather(real, "blk", axis=0, tiled=True)
    real_dist = pair_dist(home, home_sq, piece)
    term, real_weight = home_term(home, real_dist, piece, inv_r)
    sums = carry[0] + term
    loss_part = carry[1] + 2.0 * jnp.sum(real_dist) * inv_g * inv_r
    own_rows = lax.psum_scatter(sums, ("pair", "sub"), scatter_dimension=0, tiled=True)
    total_loss = lax.psum(loss_part, ("blk", "pair", "sub"))
    return (own_rows + partner, total_loss.reshape(1))


def solution(mesh):
    sizes = tuple(mesh.shape[axis] for axis in AXES)
    shards = functools.partial(small_shards, sizes) if sizes == (4, 2, 2) else large_shards
    in_specs = (
        P(("groups", "blk", "pair", "sub"), None),
        P(("groups", "blk", "pair", "sub"), None),
    )
    out_specs = (P(("groups", "blk", "pair", "sub"), None), P("groups"))
    return jax.shard_map(shards, mesh=mesh, in_specs=in_specs, out_specs=out_specs, check_vma=False)
```

```python
import functools

import jax
import jax.numpy as jnp
from jax import lax
from jax.experimental import pallas as pl
from jax.experimental.pallas import tpu as pltpu
from jax.sharding import PartitionSpec as P

AXES = ("blk", "pair", "sub")
SMALL = (4, 2, 2)
EVEN_MOVES = ((('pair', 1),), (('blk', 2),), (('blk', 1),))
ODD_MOVES = ((('blk', 2),), (('blk', 1),), (('pair', 1),))
CHIP_MOVES = (("sub", 1),)
SENDS = (('a', 'O', 0), ('b', 'O', 1), ('d', 'O', 2), ('c', 'a', 1), ('e', 'a', 2), ('f', 'b', 2), ('g', 'c', 2))
STAGES = (('O',), ('a',), ('b',), ('d',), ('c',), ('e',), ('f',), ('g',))
HELD = {}


def swap_pairs(sizes, even_moves, odd_moves):
    blk, pair, sub = sizes
    pairs = []
    for z in range(blk):
        for x in range(pair):
            for s in range(sub):
                at = {"blk": z, "pair": x, "sub": s}
                for axis, flip in odd_moves if s else even_moves:
                    at[axis] ^= flip
                source = (z * pair + x) * sub + s
                target = (at["blk"] * pair + at["pair"]) * sub + at["sub"]
                pairs.append((source, target))
    return pairs


def swapped(block, sizes, even_moves, odd_moves):
    return lax.ppermute(block, AXES, swap_pairs(sizes, even_moves, odd_moves))


def joined(held, names):
    return held[names] if names in held else jnp.concatenate([held[n] for n in names])


def stage_call(news, olds, carry, g_rows, n_pairs, final):
    step = olds[0].shape[0] if olds else news[0].shape[0]
    width = news[0].shape[1]
    r_rows = step - g_rows
    n_new = sum(b.shape[0] // step for b in news) // 2
    n_old = sum(b.shape[0] // step for b in olds) // 2
    ratio = g_rows / r_rows
    inv_total = 1.0 / (g_rows * 2 * n_pairs)
    tile = 2 * g_rows
    gens_n, reals_n = n_new * tile, n_new * 2 * r_rows
    first = not olds

    def lanes_of(n, count, offset):
        row = lax.broadcasted_iota(jnp.int32, (count, 128), 0)
        lane = lax.broadcasted_iota(jnp.int32, (count, 128), 1)
        line = jnp.sum(jnp.where(lane == row + offset, n, 0.0), axis=0, keepdims=True)
        return jnp.broadcast_to(line, (8, 128))

    def fold(d):
        rows, lanes = d.shape
        return jnp.sum(d.reshape(rows // 8, 8, lanes), axis=0)

    def kernel(*refs):
        refs = list(refs)

        def take(count):
            taken = []
            while len(taken) < count:
                ref = refs.pop(0)
                taken += [(ref, at) for at in range(0, ref.shape[0], step)]
            return taken

        def gens_of(block):
            ref, at = block
            return ref[at : at + g_rows, :]

        def reals_of(block):
            ref, at = block
            return ref[at + g_rows : at + step, :]

        new, old = take(2 * n_new), take(2 * n_old)
        if not first:
            pulled_in, sums_in, norms_in = refs.pop(0), refs.pop(0), refs.pop(0)
        gens = jnp.concatenate([gens_of(b) for b in new], axis=0)
        reals = jnp.concatenate([reals_of(b) for b in new], axis=0)
        rows = jnp.concatenate([gens, reals], axis=0)
        v = rows.astype(jnp.float32)
        n_col = jnp.sum(v * v, axis=1, keepdims=True) * (1.0 / width) + 0.5
        n_col = jnp.broadcast_to(n_col, (gens_n + reals_n, 128))
        blocks_n = [
            lanes_of(n_col[i * g_rows : (i + 1) * g_rows], g_rows, 0) for i in range(2 * n_new)
        ]
        new_n = [jnp.concatenate(blocks_n[2 * i : 2 * i + 2], axis=1) for i in range(n_new)]
        lhs = rows * jnp.asarray(-2.0 / width, rows.dtype)

        def spread(rhs, n_lane, count):
            c = lax.dot_general(
                lhs[0:count], rhs, (((1,), (1,)), ((), ())), preferred_element_type=jnp.float32
            )
            lanes = c.shape[1]
            n_row = jnp.concatenate([n_col[0:count]] * pl.cdiv(lanes, 128), axis=1)[:, 0:lanes]
            n_lane = jnp.broadcast_to(n_lane[None], (count // 8, 8, lanes)).reshape(count, lanes)
            return jnp.maximum((n_row + n_lane) + c, 1.0)

        def own_part(w):
            w = w[:, 0:g_rows]
            w = jnp.concatenate([w[0:gens_n], w[gens_n:] * (-ratio)], axis=0)
            sums = lax.dot_general(
                w.astype(jnp.bfloat16),
                rows,
                (((0,), (0,)), ((), ())),
                preferred_element_type=jnp.float32,
            )
            return sums, fold(w)

        loss = jnp.zeros((8, tile), jnp.float32)
        for i in range(n_old + n_new):
            if i < n_old:
                rhs = jnp.concatenate([gens_of(old[2 * i]), gens_of(old[2 * i + 1])], axis=0)
                s = spread(rhs, norms_in[i], gens_n + reals_n)
            else:
                j = i - n_old
                s = spread(gens[j * tile : (j + 1) * tile], new_n[j], gens_n + reals_n)
            w = lax.rsqrt(s)
            if i == 0:
                pulled, w_sum = own_part(w)
            d = s * w
            times = -2.0 if i < n_old else -1.0
            loss += fold(d[0:gens_n]) * times + fold(d[gens_n:]) * (2.0 * ratio)
        if not first:
            old_reals = jnp.concatenate([reals_of(b) for b in old], axis=0)
            s = spread(old_reals, norms_in[n_pairs][:, 0 : old_reals.shape[0]], gens_n)
            d = jnp.sum(fold(s * lax.rsqrt(s)), axis=1, keepdims=True) * (2.0 * ratio)
            lane = lax.broadcasted_iota(jnp.int32, (8, tile), 1)
            loss += jnp.where(lane == 0, d, 0.0)
            pulled = pulled + pulled_in[...]
            w_sum = w_sum + sums_in[0:8, 0:128]
            loss = loss + sums_in[8:16, :]
        if final:
            grad_ref, loss_ref = refs
            line = jnp.broadcast_to(jnp.sum(w_sum, axis=0, keepdims=True), (g_rows, 128))
            row = lax.broadcasted_iota(jnp.int32, (g_rows, g_rows), 0)
            lane = lax.broadcasted_iota(jnp.int32, (g_rows, g_rows), 1)
            w_col = jnp.sum(jnp.where(row == lane, line, 0.0), axis=1, keepdims=True)
            own = gens_of(new[0] if first else old[0]).astype(jnp.float32)
            grad_ref[...] = (pulled - own * w_col) * inv_total
            loss_ref[0] = jnp.sum(loss) * (inv_total * inv_total)
        else:
            pulled_ref, sums_ref, norms_ref = refs
            pulled_ref[...] = pulled
            sums_ref[0:8, 0:128] = w_sum
            sums_ref[8:16, :] = loss
            for i in range(n_old):
                norms_ref[i] = norms_in[i]
            for i in range(n_new):
                norms_ref[n_old + i] = new_n[i]
            at = n_old * 2 * r_rows
            real_n = jnp.concatenate(
                [lanes_of(n_col[gens_n:], reals_n, at - 128 * half) for half in range(2)], axis=1
            )
            norms_ref[n_pairs] = real_n if first else real_n + norms_in[n_pairs]

    vmem = pl.BlockSpec(memory_space=pltpu.VMEM)
    f32 = functools.partial(jax.ShapeDtypeStruct, dtype=jnp.float32)
    if final:
        out_shape = (f32((g_rows, width)), f32((1,)))
        out_specs = (vmem, pl.BlockSpec(memory_space=pltpu.SMEM))
    else:
        out_shape = (f32((g_rows, width)), f32((16, tile)), f32((n_pairs + 1, 8, tile)))
        out_specs = (vmem,) * 3
    entries = (gens_n + reals_n) * ((n_old + n_new) * tile + n_old * 2 * r_rows)
    operands = [*news, *olds, *carry]
    return pl.pallas_call(
        kernel,
        out_shape=out_shape,
        in_specs=[vmem] * len(operands),
        out_specs=out_specs,
        cost_estimate=pl.CostEstimate(
            flops=int(2 * entries * width * 1), bytes_accessed=1024, transcendentals=entries
        ),
        compiler_params=pltpu.CompilerParams(vmem_limit_bytes=32 * 1024 * 1024),
    )(*operands)


def small_shards(sizes, generated, real):
    own = jnp.concatenate([generated, real], axis=0)
    g_rows, block_rows = generated.shape[0], own.shape[0]
    n_pairs = sizes[0] * sizes[1]
    lane, chip = {"O": own}, {}
    stages, seen, carry = [], [], ()

    def held_back(name, value):
        if name not in HELD:
            return value
        return lax.optimization_barrier((value, stages[HELD[name]][1]))[0]

    def run_stages():
        nonlocal seen, carry
        while len(stages) < len(STAGES) and all(n in lane for n in STAGES[len(stages)]):
            new = []
            for n in STAGES[len(stages)]:
                chip[n] = swapped(held_back("S" + n, lane[n]), sizes, CHIP_MOVES, CHIP_MOVES)
                new += [lane[n], chip[n]]
            final = len(stages) == len(STAGES) - 1
            carry = stage_call(new, seen, carry, g_rows, n_pairs, final)
            stages.append(carry)
            seen = seen + new

    run_stages()
    for name, sources, move in SENDS:
        block = held_back(name, joined(lane, sources))
        lane[name] = swapped(block, sizes, EVEN_MOVES[move], ODD_MOVES[move])
        run_stages()
    assert sum(b.shape[0] for b in seen) == 2 * n_pairs * block_rows
    return carry


def passed_along(shard, axis, by):
    size = lax.axis_size(axis)
    return lax.ppermute(shard, axis, [(i, (i + by) % size) for i in range(size)])


def pair_dist(home, home_sq, other):
    other_sq = jnp.sum(jnp.square(other.astype(jnp.float32)), axis=1)
    gram = lax.dot_general(
        home, other, (((1,), (1,)), ((), ())), preferred_element_type=jnp.float32
    )
    spread = jnp.maximum(home_sq[:, None] + other_sq[None, :] - 2.0 * gram, 0.0)
    return jnp.sqrt(spread / home.shape[1] + 1.0)


def home_term(home, dist, other, factor):
    weight = 1.0 / dist
    pulled = jnp.dot(weight.astype(jnp.bfloat16), other, preferred_element_type=jnp.float32)
    return (factor * (home.astype(jnp.float32) * jnp.sum(weight, axis=1)[:, None] - pulled), weight)


def other_term(home, weight, other, factor):
    pulled = lax.dot_general(
        weight.astype(jnp.bfloat16),
        home,
        (((0,), (0,)), ((), ())),
        preferred_element_type=jnp.float32,
    )
    return factor * (other.astype(jnp.float32) * jnp.sum(weight, axis=0)[:, None] - pulled)


def large_shards(generated, real):
    cycle_size = lax.axis_size("blk")
    half_way = cycle_size // 2
    devices_all = lax.axis_size(("blk", "pair", "sub"))
    inv_g = 1.0 / (generated.shape[0] * devices_all)
    inv_r = 1.0 / (real.shape[0] * devices_all)
    home = lax.all_gather(generated, ("pair", "sub"), axis=0, tiled=True)
    home_sq = jnp.sum(jnp.square(home.astype(jnp.float32)), axis=1)
    dist = pair_dist(home, home_sq, generated)
    sums, weight = home_term(home, dist, generated, -inv_g)
    loss_part = -jnp.sum(dist) * inv_g * inv_g

    def sym_step(index, carry):
        visitor, partner, acc_sums, acc_loss = carry
        visitor = passed_along(visitor, "blk", 1)
        step_dist = pair_dist(home, home_sq, visitor)
        term, step_weight = home_term(home, step_dist, visitor, -inv_g)
        partner = partner + other_term(home, step_weight, visitor, -inv_g)
        partner = passed_along(partner, "blk", 1)
        return (
            visitor,
            partner,
            acc_sums + term,
            acc_loss - 2.0 * jnp.sum(step_dist) * inv_g * inv_g,
        )

    start_partner = jnp.zeros(generated.shape, jnp.float32)
    visitor, partner, sums, loss_part = lax.fori_loop(
        0, half_way - 1, sym_step, (generated, start_partner, sums, loss_part)
    )
    visitor = passed_along(visitor, "blk", 1)
    last_dist = pair_dist(home, home_sq, visitor)
    term, last_weight = home_term(home, last_dist, visitor, -inv_g)
    sums = sums + term
    loss_part = loss_part - jnp.sum(last_dist) * inv_g * inv_g
    partner = passed_along(partner, "blk", cycle_size - half_way)
    carry = (sums, loss_part)
    piece = lax.all_gather(real, "blk", axis=0, tiled=True)
    real_dist = pair_dist(home, home_sq, piece)
    term, real_weight = home_term(home, real_dist, piece, inv_r)
    sums = carry[0] + term
    loss_part = carry[1] + 2.0 * jnp.sum(real_dist) * inv_g * inv_r
    own_rows = lax.psum_scatter(sums, ("pair", "sub"), scatter_dimension=0, tiled=True)
    total_loss = lax.psum(loss_part, ("blk", "pair", "sub"))
    return (own_rows + partner, total_loss.reshape(1))


def solution(mesh):
    sizes = tuple(mesh.shape[axis] for axis in AXES)
    shards = functools.partial(small_shards, sizes) if sizes == SMALL else large_shards
    in_specs = (
        P(("groups", "blk", "pair", "sub"), None),
        P(("groups", "blk", "pair", "sub"), None),
    )
    out_specs = (P(("groups", "blk", "pair", "sub"), None), P("groups"))
    return jax.shard_map(shards, mesh=mesh, in_specs=in_specs, out_specs=out_specs, check_vma=False)
```

```python
import functools

import jax
import jax.numpy as jnp
from jax import lax
from jax.experimental import pallas as pl
from jax.experimental.pallas import tpu as pltpu
from jax.sharding import PartitionSpec as P

AXES = ("blk", "pair", "sub")
SMALL = (4, 2, 2)
EVEN_MOVES = (('pair', 1), ('blk', 2), ('blk', 1))
ODD_MOVES = (('blk', 2), ('blk', 1), ('pair', 1))
CHIP_MOVES = (("sub", 1),)
SENDS = (('a', 'O', 0), ('b', 'O', 1), ('d', 'O', 2), ('c', 'a', 1), ('e', 'a', 2), ('f', 'b', 2), ('g', 'c', 2))
STAGES = (('O',), ('a', 'b'), ('d', 'e'), ('c', 'f'), ('g',))


def swap_pairs(sizes, even_moves, odd_moves):
    blk, pair, sub = sizes
    pairs = []
    for z in range(blk):
        for x in range(pair):
            for s in range(sub):
                at = {"blk": z, "pair": x, "sub": s}
                for axis, flip in odd_moves if s else even_moves:
                    at[axis] ^= flip
                source = (z * pair + x) * sub + s
                target = (at["blk"] * pair + at["pair"]) * sub + at["sub"]
                pairs.append((source, target))
    return pairs


def swapped(block, sizes, even_moves, odd_moves):
    return lax.ppermute(block, AXES, swap_pairs(sizes, even_moves, odd_moves))


def stage_call(news, olds, carry, g_rows, n_pairs, final):
    step = olds[0].shape[0] if olds else news[0].shape[0]
    width = news[0].shape[1]
    r_rows = step - g_rows
    n_new = sum(b.shape[0] // step for b in news) // 2
    n_old = sum(b.shape[0] // step for b in olds) // 2
    ratio = g_rows / r_rows
    inv_total = 1.0 / (g_rows * 2 * n_pairs)
    tile = 2 * g_rows
    gens_n, reals_n = n_new * tile, n_new * 2 * r_rows
    first = not olds

    def lanes_of(n, count, offset):
        row = lax.broadcasted_iota(jnp.int32, (count, 128), 0)
        lane = lax.broadcasted_iota(jnp.int32, (count, 128), 1)
        line = jnp.sum(jnp.where(lane == row + offset, n, 0.0), axis=0, keepdims=True)
        return jnp.broadcast_to(line, (8, 128))

    def fold(d):
        rows, lanes = d.shape
        return jnp.sum(d.reshape(rows // 8, 8, lanes), axis=0)

    def kernel(*refs):
        refs = list(refs)

        def take(count):
            taken = []
            while len(taken) < count:
                ref = refs.pop(0)
                taken += [(ref, at) for at in range(0, ref.shape[0], step)]
            return taken

        def gens_of(block):
            ref, at = block
            return ref[at : at + g_rows, :]

        def reals_of(block):
            ref, at = block
            return ref[at + g_rows : at + step, :]

        new, old = take(2 * n_new), take(2 * n_old)
        if not first:
            pulled_in, sums_in, norms_in = refs.pop(0), refs.pop(0), refs.pop(0)
        gens = jnp.concatenate([gens_of(b) for b in new], axis=0)
        reals = jnp.concatenate([reals_of(b) for b in new], axis=0)
        rows = jnp.concatenate([gens, reals], axis=0)
        v = rows.astype(jnp.float32)
        n_col = jnp.sum(v * v, axis=1, keepdims=True) * (1.0 / width) + 0.5
        n_col = jnp.broadcast_to(n_col, (gens_n + reals_n, 128))
        blocks_n = [
            lanes_of(n_col[i * g_rows : (i + 1) * g_rows], g_rows, 0) for i in range(2 * n_new)
        ]
        new_n = [jnp.concatenate(blocks_n[2 * i : 2 * i + 2], axis=1) for i in range(n_new)]
        lhs = rows * jnp.asarray(-2.0 / width, rows.dtype)

        def spread(rhs, n_lane, begin, end):
            c = lax.dot_general(
                lhs[begin:end], rhs, (((1,), (1,)), ((), ())), preferred_element_type=jnp.float32
            )
            count, lanes = c.shape
            n_row = jnp.concatenate([n_col[begin:end]] * pl.cdiv(lanes, 128), axis=1)[:, 0:lanes]
            n_lane = jnp.broadcast_to(n_lane[None], (count // 8, 8, lanes)).reshape(count, lanes)
            return jnp.maximum((n_row + n_lane) + c, 1.0)

        def own_part(w):
            w = w[:, 0:g_rows]
            w = jnp.concatenate([w[0:gens_n], w[gens_n:] * (-ratio)], axis=0)
            sums = lax.dot_general(
                w.astype(jnp.bfloat16),
                rows,
                (((0,), (0,)), ((), ())),
                preferred_element_type=jnp.float32,
            )
            return sums, fold(w)

        loss = jnp.zeros((8, tile), jnp.float32)
        for i in range(n_old + n_new):
            if i < n_old:
                begin = 0
                rhs = jnp.concatenate([gens_of(old[2 * i]), gens_of(old[2 * i + 1])], axis=0)
                n_lane = norms_in[i]
            else:
                begin = (i - n_old) * tile
                rhs = gens[begin : begin + tile]
                n_lane = new_n[i - n_old]
            s = spread(rhs, n_lane, begin, gens_n + reals_n)
            w = lax.rsqrt(s)
            if i == 0:
                pulled, w_sum = own_part(w)
            d = s * w
            reals_at = gens_n - begin
            loss += fold(d[reals_at:]) * (2.0 * ratio)
            once = 0 if i < n_old else tile
            if once:
                loss += fold(d[0:once]) * -1.0
            if once < reals_at:
                loss += fold(d[once:reals_at]) * -2.0
        if not first:
            old_reals = jnp.concatenate([reals_of(b) for b in old], axis=0)
            s = spread(old_reals, norms_in[n_pairs][:, 0 : old_reals.shape[0]], 0, gens_n)
            d = jnp.sum(fold(s * lax.rsqrt(s)), axis=1, keepdims=True) * (2.0 * ratio)
            lane = lax.broadcasted_iota(jnp.int32, (8, tile), 1)
            loss += jnp.where(lane == 0, d, 0.0)
            pulled = pulled + pulled_in[...]
            w_sum = w_sum + sums_in[0:8, 0:128]
            loss = loss + sums_in[8:16, :]
        if final:
            grad_ref, loss_ref = refs
            line = jnp.broadcast_to(jnp.sum(w_sum, axis=0, keepdims=True), (g_rows, 128))
            row = lax.broadcasted_iota(jnp.int32, (g_rows, g_rows), 0)
            lane = lax.broadcasted_iota(jnp.int32, (g_rows, g_rows), 1)
            w_col = jnp.sum(jnp.where(row == lane, line, 0.0), axis=1, keepdims=True)
            own = gens_of(new[0] if first else old[0]).astype(jnp.float32)
            grad_ref[...] = (pulled - own * w_col) * inv_total
            loss_ref[0] = jnp.sum(loss) * (inv_total * inv_total)
        else:
            pulled_ref, sums_ref, norms_ref = refs
            pulled_ref[...] = pulled
            sums_ref[0:8, 0:128] = w_sum
            sums_ref[8:16, :] = loss
            for i in range(n_old):
                norms_ref[i] = norms_in[i]
            for i in range(n_new):
                norms_ref[n_old + i] = new_n[i]
            at = n_old * 2 * r_rows
            real_n = jnp.concatenate(
                [lanes_of(n_col[gens_n:], reals_n, at - 128 * half) for half in range(2)], axis=1
            )
            norms_ref[n_pairs] = real_n if first else real_n + norms_in[n_pairs]

    vmem = pl.BlockSpec(memory_space=pltpu.VMEM)
    f32 = functools.partial(jax.ShapeDtypeStruct, dtype=jnp.float32)
    if final:
        out_shape = (f32((g_rows, width)), f32((1,)))
        out_specs = (vmem, pl.BlockSpec(memory_space=pltpu.SMEM))
    else:
        out_shape = (f32((g_rows, width)), f32((16, tile)), f32((n_pairs + 1, 8, tile)))
        out_specs = (vmem,) * 3
    entries = (gens_n + reals_n) * ((n_old + n_new) * tile + n_old * 2 * r_rows)
    operands = [*news, *olds, *carry]
    return pl.pallas_call(
        kernel,
        out_shape=out_shape,
        in_specs=[vmem] * len(operands),
        out_specs=out_specs,
        cost_estimate=pl.CostEstimate(
            flops=int(2 * entries * width * 1), bytes_accessed=1024, transcendentals=entries
        ),
        compiler_params=pltpu.CompilerParams(vmem_limit_bytes=32 * 1024 * 1024),
    )(*operands)


def small_shards(sizes, generated, real):
    own = jnp.concatenate([generated, real], axis=0)
    g_rows, block_rows = generated.shape[0], own.shape[0]
    n_pairs = sizes[0] * sizes[1]
    lane = {"O": own}
    for name, source, move in SENDS:
        even, odd = EVEN_MOVES[move], ODD_MOVES[move]
        lane[name] = swapped(lane[source], sizes, (even,), (odd,))
    seen, carry = [], ()
    for names in STAGES:
        news = []
        for name in names:
            news += [lane[name], swapped(lane[name], sizes, CHIP_MOVES, CHIP_MOVES)]
        carry = stage_call(news, seen, carry, g_rows, n_pairs, names == STAGES[-1])
        seen = seen + news
    assert sum(b.shape[0] for b in seen) == 2 * n_pairs * block_rows
    return carry


def passed_along(shard, axis, by):
    size = lax.axis_size(axis)
    return lax.ppermute(shard, axis, [(i, (i + by) % size) for i in range(size)])


def pair_dist(home, home_sq, other):
    other_sq = jnp.sum(jnp.square(other.astype(jnp.float32)), axis=1)
    gram = lax.dot_general(
        home, other, (((1,), (1,)), ((), ())), preferred_element_type=jnp.float32
    )
    spread = jnp.maximum(home_sq[:, None] + other_sq[None, :] - 2.0 * gram, 0.0)
    return jnp.sqrt(spread / home.shape[1] + 1.0)


def home_term(home, dist, other, factor):
    weight = 1.0 / dist
    pulled = jnp.dot(weight.astype(jnp.bfloat16), other, preferred_element_type=jnp.float32)
    return (factor * (home.astype(jnp.float32) * jnp.sum(weight, axis=1)[:, None] - pulled), weight)


def other_term(home, weight, other, factor):
    pulled = lax.dot_general(
        weight.astype(jnp.bfloat16),
        home,
        (((0,), (0,)), ((), ())),
        preferred_element_type=jnp.float32,
    )
    return factor * (other.astype(jnp.float32) * jnp.sum(weight, axis=0)[:, None] - pulled)


def large_shards(generated, real):
    cycle_size = lax.axis_size("blk")
    half_way = cycle_size // 2
    devices_all = lax.axis_size(("blk", "pair", "sub"))
    inv_g = 1.0 / (generated.shape[0] * devices_all)
    inv_r = 1.0 / (real.shape[0] * devices_all)
    home = lax.all_gather(generated, ("pair", "sub"), axis=0, tiled=True)
    home_sq = jnp.sum(jnp.square(home.astype(jnp.float32)), axis=1)
    dist = pair_dist(home, home_sq, generated)
    sums, weight = home_term(home, dist, generated, -inv_g)
    loss_part = -jnp.sum(dist) * inv_g * inv_g

    def sym_step(index, carry):
        visitor, partner, acc_sums, acc_loss = carry
        visitor = passed_along(visitor, "blk", 1)
        step_dist = pair_dist(home, home_sq, visitor)
        term, step_weight = home_term(home, step_dist, visitor, -inv_g)
        partner = partner + other_term(home, step_weight, visitor, -inv_g)
        partner = passed_along(partner, "blk", 1)
        return (
            visitor,
            partner,
            acc_sums + term,
            acc_loss - 2.0 * jnp.sum(step_dist) * inv_g * inv_g,
        )

    start_partner = jnp.zeros(generated.shape, jnp.float32)
    visitor, partner, sums, loss_part = lax.fori_loop(
        0, half_way - 1, sym_step, (generated, start_partner, sums, loss_part)
    )
    visitor = passed_along(visitor, "blk", 1)
    last_dist = pair_dist(home, home_sq, visitor)
    term, last_weight = home_term(home, last_dist, visitor, -inv_g)
    sums = sums + term
    loss_part = loss_part - jnp.sum(last_dist) * inv_g * inv_g
    partner = passed_along(partner, "blk", cycle_size - half_way)
    carry = (sums, loss_part)
    piece = lax.all_gather(real, "blk", axis=0, tiled=True)
    real_dist = pair_dist(home, home_sq, piece)
    term, real_weight = home_term(home, real_dist, piece, inv_r)
    sums = carry[0] + term
    loss_part = carry[1] + 2.0 * jnp.sum(real_dist) * inv_g * inv_r
    own_rows = lax.psum_scatter(sums, ("pair", "sub"), scatter_dimension=0, tiled=True)
    total_loss = lax.psum(loss_part, ("blk", "pair", "sub"))
    return (own_rows + partner, total_loss.reshape(1))


def solution(mesh):
    sizes = tuple(mesh.shape[axis] for axis in AXES)
    shards = functools.partial(small_shards, sizes) if sizes == SMALL else large_shards
    in_specs = (
        P(("groups", "blk", "pair", "sub"), None),
        P(("groups", "blk", "pair", "sub"), None),
    )
    out_specs = (P(("groups", "blk", "pair", "sub"), None), P("groups"))
    return jax.shard_map(shards, mesh=mesh, in_specs=in_specs, out_specs=out_specs, check_vma=False)
```

```python
import functools

import jax
import jax.numpy as jnp
from jax import lax
from jax.experimental import pallas as pl
from jax.experimental.pallas import tpu as pltpu
from jax.sharding import PartitionSpec as P

AXES = ("blk", "pair", "sub")
SMALL = (4, 2, 2)
EVEN_MOVES = (('pair', 1), ('blk', 2), ('blk', 1))
ODD_MOVES = (('blk', 2), ('blk', 1), ('pair', 1))
CHIP_MOVES = (("sub", 1),)
SENDS = (('a', 'O', 0), ('b', 'O', 1), ('d', 'O', 2), ('c', 'a', 1), ('e', 'a', 2), ('f', 'b', 2), ('g', 'c', 2))
STAGES = (('O',), ('a', 'b'), ('d', 'c'), ('e', 'f'), ('g',))
STAGE_COSTS = (0.6, 1.0, 1.5, 1.0, 6.0)


def swap_pairs(sizes, even_moves, odd_moves):
    blk, pair, sub = sizes
    pairs = []
    for z in range(blk):
        for x in range(pair):
            for s in range(sub):
                at = {"blk": z, "pair": x, "sub": s}
                for axis, flip in odd_moves if s else even_moves:
                    at[axis] ^= flip
                source = (z * pair + x) * sub + s
                target = (at["blk"] * pair + at["pair"]) * sub + at["sub"]
                pairs.append((source, target))
    return pairs


def swapped(block, sizes, even_moves, odd_moves):
    return lax.ppermute(block, AXES, swap_pairs(sizes, even_moves, odd_moves))


def stage_call(news, olds, carry, g_rows, n_pairs, final, cost):
    step = olds[0].shape[0] if olds else news[0].shape[0]
    width = news[0].shape[1]
    r_rows = step - g_rows
    n_new = sum(b.shape[0] // step for b in news) // 2
    n_old = sum(b.shape[0] // step for b in olds) // 2
    ratio = g_rows / r_rows
    inv_total = 1.0 / (g_rows * 2 * n_pairs)
    tile = 2 * g_rows
    gens_n, reals_n = n_new * tile, n_new * 2 * r_rows
    first = not olds

    def lanes_of(n, count, offset):
        row = lax.broadcasted_iota(jnp.int32, (count, 128), 0)
        lane = lax.broadcasted_iota(jnp.int32, (count, 128), 1)
        line = jnp.sum(jnp.where(lane == row + offset, n, 0.0), axis=0, keepdims=True)
        return jnp.broadcast_to(line, (8, 128))

    def fold(d):
        rows, lanes = d.shape
        return jnp.sum(d.reshape(rows // 8, 8, lanes), axis=0)

    def kernel(*refs):
        refs = list(refs)

        def take(count):
            taken = []
            while len(taken) < count:
                ref = refs.pop(0)
                taken += [(ref, at) for at in range(0, ref.shape[0], step)]
            return taken

        def gens_of(block):
            ref, at = block
            return ref[at : at + g_rows, :]

        def reals_of(block):
            ref, at = block
            return ref[at + g_rows : at + step, :]

        new, old = take(2 * n_new), take(2 * n_old)
        if not first:
            pulled_in, sums_in, norms_in = refs.pop(0), refs.pop(0), refs.pop(0)
        gens = jnp.concatenate([gens_of(b) for b in new], axis=0)
        reals = jnp.concatenate([reals_of(b) for b in new], axis=0)
        rows = jnp.concatenate([gens, reals], axis=0)
        v = rows.astype(jnp.float32)
        n_col = jnp.sum(v * v, axis=1, keepdims=True) * (1.0 / width) + 0.5
        n_col = jnp.broadcast_to(n_col, (gens_n + reals_n, 128))
        blocks_n = [
            lanes_of(n_col[i * g_rows : (i + 1) * g_rows], g_rows, 0) for i in range(2 * n_new)
        ]
        new_n = [jnp.concatenate(blocks_n[2 * i : 2 * i + 2], axis=1) for i in range(n_new)]
        lhs = rows * jnp.asarray(-2.0 / width, rows.dtype)

        def spread(rhs, n_lane, begin, end):
            c = lax.dot_general(
                lhs[begin:end], rhs, (((1,), (1,)), ((), ())), preferred_element_type=jnp.float32
            )
            count, lanes = c.shape
            n_row = jnp.concatenate([n_col[begin:end]] * pl.cdiv(lanes, 128), axis=1)[:, 0:lanes]
            n_lane = jnp.broadcast_to(n_lane[None], (count // 8, 8, lanes)).reshape(count, lanes)
            return jnp.maximum((n_row + n_lane) + c, 1.0)

        def own_part(w):
            w = w[:, 0:g_rows]
            w = jnp.concatenate([w[0:gens_n], w[gens_n:] * (-ratio)], axis=0)
            sums = lax.dot_general(
                w.astype(jnp.bfloat16),
                rows,
                (((0,), (0,)), ((), ())),
                preferred_element_type=jnp.float32,
            )
            return sums, fold(w)

        loss = jnp.zeros((8, tile), jnp.float32)
        for i in range(n_old + n_new):
            if i < n_old:
                begin = 0
                rhs = jnp.concatenate([gens_of(old[2 * i]), gens_of(old[2 * i + 1])], axis=0)
                n_lane = norms_in[i]
            else:
                begin = (i - n_old) * tile
                rhs = gens[begin : begin + tile]
                n_lane = new_n[i - n_old]
            s = spread(rhs, n_lane, begin, gens_n + reals_n)
            w = lax.rsqrt(s)
            if i == 0:
                pulled, w_sum = own_part(w)
            d = s * w
            reals_at = gens_n - begin
            loss += fold(d[reals_at:]) * (2.0 * ratio)
            once = 0 if i < n_old else tile
            if once:
                loss += fold(d[0:once]) * -1.0
            if once < reals_at:
                loss += fold(d[once:reals_at]) * -2.0
        if not first:
            old_reals = jnp.concatenate([reals_of(b) for b in old], axis=0)
            s = spread(old_reals, norms_in[n_pairs][:, 0 : old_reals.shape[0]], 0, gens_n)
            d = jnp.sum(fold(s * lax.rsqrt(s)), axis=1, keepdims=True) * (2.0 * ratio)
            lane = lax.broadcasted_iota(jnp.int32, (8, tile), 1)
            loss += jnp.where(lane == 0, d, 0.0)
            pulled = pulled + pulled_in[...]
            w_sum = w_sum + sums_in[0:8, 0:128]
            loss = loss + sums_in[8:16, :]
        if final:
            grad_ref, loss_ref = refs
            line = jnp.broadcast_to(jnp.sum(w_sum, axis=0, keepdims=True), (g_rows, 128))
            row = lax.broadcasted_iota(jnp.int32, (g_rows, g_rows), 0)
            lane = lax.broadcasted_iota(jnp.int32, (g_rows, g_rows), 1)
            w_col = jnp.sum(jnp.where(row == lane, line, 0.0), axis=1, keepdims=True)
            own = gens_of(new[0] if first else old[0]).astype(jnp.float32)
            grad_ref[...] = (pulled - own * w_col) * inv_total
            loss_ref[0] = jnp.sum(loss) * (inv_total * inv_total)
        else:
            pulled_ref, sums_ref, norms_ref = refs
            pulled_ref[...] = pulled
            sums_ref[0:8, 0:128] = w_sum
            sums_ref[8:16, :] = loss
            for i in range(n_old):
                norms_ref[i] = norms_in[i]
            for i in range(n_new):
                norms_ref[n_old + i] = new_n[i]
            at = n_old * 2 * r_rows
            real_n = jnp.concatenate(
                [lanes_of(n_col[gens_n:], reals_n, at - 128 * half) for half in range(2)], axis=1
            )
            norms_ref[n_pairs] = real_n if first else real_n + norms_in[n_pairs]

    vmem = pl.BlockSpec(memory_space=pltpu.VMEM)
    f32 = functools.partial(jax.ShapeDtypeStruct, dtype=jnp.float32)
    if final:
        out_shape = (f32((g_rows, width)), f32((1,)))
        out_specs = (vmem, pl.BlockSpec(memory_space=pltpu.SMEM))
    else:
        out_shape = (f32((g_rows, width)), f32((16, tile)), f32((n_pairs + 1, 8, tile)))
        out_specs = (vmem,) * 3
    entries = (gens_n + reals_n) * ((n_old + n_new) * tile + n_old * 2 * r_rows)
    operands = [*news, *olds, *carry]
    return pl.pallas_call(
        kernel,
        out_shape=out_shape,
        in_specs=[vmem] * len(operands),
        out_specs=out_specs,
        cost_estimate=pl.CostEstimate(
            flops=int(2 * entries * width * cost), bytes_accessed=1024, transcendentals=entries
        ),
        compiler_params=pltpu.CompilerParams(vmem_limit_bytes=32 * 1024 * 1024),
    )(*operands)


def small_shards(sizes, generated, real):
    own = jnp.concatenate([generated, real], axis=0)
    g_rows, block_rows = generated.shape[0], own.shape[0]
    n_pairs = sizes[0] * sizes[1]
    lane = {"O": own}
    for name, source, move in SENDS:
        even, odd = EVEN_MOVES[move], ODD_MOVES[move]
        lane[name] = swapped(lane[source], sizes, (even,), (odd,))
    seen, carry = [], ()
    for names, cost in zip(STAGES, STAGE_COSTS, strict=True):
        news = []
        for name in names:
            news += [lane[name], swapped(lane[name], sizes, CHIP_MOVES, CHIP_MOVES)]
        final = names == STAGES[-1]
        carry = stage_call(news, seen, carry, g_rows, n_pairs, final, cost)
        seen = seen + news
    assert sum(b.shape[0] for b in seen) == 2 * n_pairs * block_rows
    return carry


def passed_along(shard, axis, by):
    size = lax.axis_size(axis)
    return lax.ppermute(shard, axis, [(i, (i + by) % size) for i in range(size)])


def pair_dist(home, home_sq, other):
    other_sq = jnp.sum(jnp.square(other.astype(jnp.float32)), axis=1)
    gram = lax.dot_general(
        home, other, (((1,), (1,)), ((), ())), preferred_element_type=jnp.float32
    )
    spread = jnp.maximum(home_sq[:, None] + other_sq[None, :] - 2.0 * gram, 0.0)
    return jnp.sqrt(spread / home.shape[1] + 1.0)


def home_term(home, dist, other, factor):
    weight = 1.0 / dist
    pulled = jnp.dot(weight.astype(jnp.bfloat16), other, preferred_element_type=jnp.float32)
    return (factor * (home.astype(jnp.float32) * jnp.sum(weight, axis=1)[:, None] - pulled), weight)


def other_term(home, weight, other, factor):
    pulled = lax.dot_general(
        weight.astype(jnp.bfloat16),
        home,
        (((0,), (0,)), ((), ())),
        preferred_element_type=jnp.float32,
    )
    return factor * (other.astype(jnp.float32) * jnp.sum(weight, axis=0)[:, None] - pulled)


def large_shards(generated, real):
    cycle_size = lax.axis_size("blk")
    half_way = cycle_size // 2
    devices_all = lax.axis_size(("blk", "pair", "sub"))
    inv_g = 1.0 / (generated.shape[0] * devices_all)
    inv_r = 1.0 / (real.shape[0] * devices_all)
    home = lax.all_gather(generated, ("pair", "sub"), axis=0, tiled=True)
    home_sq = jnp.sum(jnp.square(home.astype(jnp.float32)), axis=1)
    dist = pair_dist(home, home_sq, generated)
    sums, weight = home_term(home, dist, generated, -inv_g)
    loss_part = -jnp.sum(dist) * inv_g * inv_g

    def sym_step(index, carry):
        visitor, partner, acc_sums, acc_loss = carry
        visitor = passed_along(visitor, "blk", 1)
        step_dist = pair_dist(home, home_sq, visitor)
        term, step_weight = home_term(home, step_dist, visitor, -inv_g)
        partner = partner + other_term(home, step_weight, visitor, -inv_g)
        partner = passed_along(partner, "blk", 1)
        return (
            visitor,
            partner,
            acc_sums + term,
            acc_loss - 2.0 * jnp.sum(step_dist) * inv_g * inv_g,
        )

    start_partner = jnp.zeros(generated.shape, jnp.float32)
    visitor, partner, sums, loss_part = lax.fori_loop(
        0, half_way - 1, sym_step, (generated, start_partner, sums, loss_part)
    )
    visitor = passed_along(visitor, "blk", 1)
    last_dist = pair_dist(home, home_sq, visitor)
    term, last_weight = home_term(home, last_dist, visitor, -inv_g)
    sums = sums + term
    loss_part = loss_part - jnp.sum(last_dist) * inv_g * inv_g
    partner = passed_along(partner, "blk", cycle_size - half_way)
    carry = (sums, loss_part)
    piece = lax.all_gather(real, "blk", axis=0, tiled=True)
    real_dist = pair_dist(home, home_sq, piece)
    term, real_weight = home_term(home, real_dist, piece, inv_r)
    sums = carry[0] + term
    loss_part = carry[1] + 2.0 * jnp.sum(real_dist) * inv_g * inv_r
    own_rows = lax.psum_scatter(sums, ("pair", "sub"), scatter_dimension=0, tiled=True)
    total_loss = lax.psum(loss_part, ("blk", "pair", "sub"))
    return (own_rows + partner, total_loss.reshape(1))


def solution(mesh):
    sizes = tuple(mesh.shape[axis] for axis in AXES)
    shards = functools.partial(small_shards, sizes) if sizes == SMALL else large_shards
    in_specs = (
        P(("groups", "blk", "pair", "sub"), None),
        P(("groups", "blk", "pair", "sub"), None),
    )
    out_specs = (P(("groups", "blk", "pair", "sub"), None), P("groups"))
    return jax.shard_map(shards, mesh=mesh, in_specs=in_specs, out_specs=out_specs, check_vma=False)
```
